256 devices in a mesh: row: 8 (over z), col: 32 (over y, x, core).
Axes of the slice: x: 4, y: 4, z: 8, core: 2. Of those that a mesh axis runs over, the one named last changes fastest.
Arguments:
- slab_rows: int32 [256], P(('row', 'col')), may hold values from 1 to 256, 40960 in all
- guess: float32 [256, 256, 256], P(('row', 'col')), may hold values from -6 to 6
- right_side: float32 [256, 256, 256], P(('row', 'col')), may hold values from -6 to 6
- diagonal: float32 [256, 256, 256], P(('row', 'col')), may hold values from 2 to 6
- rates: float32 [8, 2304], P('row', 'col'), may hold values from 0.2 to 2
- term_source: int32 [8, 2304], P('row', 'col'), may hold values from 0 to 7
- term_target: int32 [8, 2304], P('row', 'col'), may hold values from 0 to 31
- term_left: int32 [8, 2304], P('row', 'col'), may hold values from 0 to 7
- term_right: int32 [8, 2304], P('row', 'col'), may hold values from 0 to 7
- left_factors: bfloat16 [8, 256, 256], replicated, may hold values from -0.375 to 0.375
- right_factors: bfloat16 [8, 256, 256], replicated, may hold values from -0.375 to 0.375
Outputs:
- iterate: float32 [256, 256, 256], P(('row', 'col'))
The draws below stay inside these ranges and needn't reach their ends.
Inputs may be any that keep to these rules, and one draw needn't show every extreme that they name: `slab_rows`: each value is the reachable row count of one slab; the values sum to 40960 and the largest is exactly 256.
All inputs are finite; a program needn't handle non-finite values. No bound on the sum of `slab_rows` on one device may be relied on, other than what follows from the above.
Results may differ from the reference program's by a relative error of at most 0.0057.
Values may be sent and summed in bfloat16 or wider, within the bound.
A program may use at most 128 MiB of HBM per device.

```python
import math
import jax
import jax.numpy as jnp
import numpy as np
from jax import lax

SPACE = 256
MAC_DEV = 1
TERMS_DEV = 72
FACTORS = 8
MACROS = 256
LIVE = 40960
N_ROW = 8
N_COL = 32


def set_ends(result, rng, low, high):
    extent = result.shape
    spot = [jax.random.randint(jax.random.fold_in(rng, axis), (), 0, extent[axis]) for axis in range(len(extent))]
    result = result.at[tuple(spot)].set(low)
    longest = extent.index(max(extent))
    spot[longest] = (spot[longest] + 1) % extent[longest]
    return result.at[tuple(spot)].set(high)


def shard_levels(rng, extent, pieces, smallest, top_value):
    factor_of = 1.0
    for dim, blocks in pieces:
        steps = jax.random.uniform(jax.random.fold_in(jax.random.fold_in(rng, 6), dim), (blocks,), jnp.float32, smallest / len(pieces), top_value / len(pieces))
        factor_of = factor_of * jnp.repeat(jnp.exp(steps), extent[dim] // blocks).reshape((-1,) + (1,) * (len(extent) - 1 - dim))
    return factor_of


def split_up(number_of, total, most, lean):
    loads = [(1 << 20) // math.isqrt(standing ** lean) + 1 for standing in range(2, number_of + 1)]
    rest, holding = total - most - (number_of - 1), [1] * (number_of - 1)
    while rest > 0:
        free = [i for i in range(number_of - 1) if holding[i] < most]
        mass, budget = sum([loads[i] for i in free]), rest
        for i in free:
            extra = min(most - holding[i], max(1, budget * loads[i] // mass), rest)
            holding[i] = holding[i] + extra
            rest = rest - extra
    return np.array([most] + holding)


def uneven(own_key, number_of, total, bound, slope):
    if number_of == 2:
        one = jax.random.randint(own_key, (), max(1, total - bound), min(bound, total - 1) + 1)
        return jnp.stack([one, total - one])
    tallies = jnp.asarray(split_up(number_of, total, bound, slope), jnp.int32)
    twos = (number_of - 1) // 2
    giver, taker = tallies[1:1 + 2 * twos:2], tallies[2:2 + 2 * twos:2]
    slack = jnp.minimum(giver - 1, bound - taker)
    passed = jax.random.randint(jax.random.fold_in(own_key, 1), (twos,), 0, 1 << 20) % (slack + 1)
    tallies = tallies.at[1:1 + 2 * twos:2].set(giver - passed).at[2:2 + 2 * twos:2].set(taker + passed)
    return tallies[jax.random.permutation(jax.random.fold_in(own_key, 2), number_of)]


def bell_draw(rng, shape, spread, reach, shards=(), kind=jnp.bfloat16):
    entries = jax.random.normal(rng, shape, jnp.float32) * spread
    if len(shards) > 0:
        entries = shard_levels(rng, shape, shards, -0.22, 0.18) * entries
    return jnp.clip(entries, min=-reach, max=reach).astype(kind)


def setup_inputs(seed: int = 0) -> dict:
    seeds = jax.random.split(jax.random.key(seed), 12)
    slab_rows = uneven(seeds[0], MACROS, LIVE, SPACE, 2).astype(jnp.int32)
    guess = bell_draw(seeds[1], (MACROS, SPACE, SPACE), 1.0, 6.0, ((0, 256),), jnp.float32)
    right_side = bell_draw(seeds[2], (MACROS, SPACE, SPACE), 1.0, 6.0, ((0, 256),), jnp.float32)
    diagonal = jnp.clip(2.0 + 4.0 * jax.random.uniform(seeds[3], (MACROS, SPACE, SPACE), jnp.float32) ** shard_levels(seeds[3], (MACROS, SPACE, SPACE), ((0, 256),), -0.2, 0.2), 2.0, 6.0)
    rates = jnp.clip(jnp.exp(math.log(2.0) - 2.3025851 * jax.random.uniform(seeds[4], (N_ROW, N_COL * TERMS_DEV), jnp.float32) ** shard_levels(seeds[4], (N_ROW, N_COL * TERMS_DEV), ((0, 8), (1, 32)), -0.2, 0.2)), 0.2, 2.0)
    term_source = set_ends(jax.random.randint(seeds[5], (N_ROW, N_COL * TERMS_DEV), 0, N_ROW * MAC_DEV), jax.random.fold_in(seeds[5], 1), 0, (N_ROW * MAC_DEV) - 1).astype(jnp.int32)
    term_target = set_ends(jax.random.randint(seeds[6], (N_ROW, N_COL * TERMS_DEV), 0, N_COL * MAC_DEV), jax.random.fold_in(seeds[6], 1), 0, (N_COL * MAC_DEV) - 1).astype(jnp.int32)
    term_left = set_ends(jax.random.randint(seeds[7], (N_ROW, N_COL * TERMS_DEV), 0, FACTORS), jax.random.fold_in(seeds[7], 1), 0, FACTORS - 1).astype(jnp.int32)
    term_right = set_ends(jax.random.randint(seeds[8], (N_ROW, N_COL * TERMS_DEV), 0, FACTORS), jax.random.fold_in(seeds[8], 1), 0, FACTORS - 1).astype(jnp.int32)
    left_factors = bell_draw(seeds[9], (FACTORS, SPACE, SPACE), SPACE ** -0.5, 0.375)
    right_factors = bell_draw(seeds[10], (FACTORS, SPACE, SPACE), SPACE ** -0.5, 0.375)
    return {"slab_rows": slab_rows, "guess": guess, "right_side": right_side, "diagonal": diagonal, "rates": rates, "term_source": term_source, "term_target": term_target, "term_left": term_left, "term_right": term_right, "left_factors": left_factors, "right_factors": right_factors}


def term_product(slab, left, right):
    inner = lax.dot_general(slab, right, (((1,), (1,)), ((), ())), preferred_element_type=jnp.float32).astype(jnp.bfloat16)
    return jnp.dot(left, inner, preferred_element_type=jnp.float32)


def reference(slab_rows, guess, right_side, diagonal, rates, term_source, term_target, term_left, term_right, left_factors, right_factors):
    group = N_COL * MAC_DEV
    positions = jnp.arange(N_COL * TERMS_DEV, dtype=jnp.int32)
    column = (positions // TERMS_DEV)[None, :]
    rowidx = jnp.arange(N_ROW, dtype=jnp.int32)[:, None]
    glob_src = (term_source // MAC_DEV) * group + column * MAC_DEV + term_source % MAC_DEV
    glob_tgt = rowidx * group + term_target
    flat = (rates.reshape(-1), glob_src.reshape(-1).astype(jnp.int32), glob_tgt.reshape(-1).astype(jnp.int32), term_left.reshape(-1), term_right.reshape(-1))
    mask = (jnp.arange(SPACE, dtype=jnp.int32)[None, :, None] < slab_rows[:, None, None]).astype(jnp.float32)
    state = guess
    for step in range(2):
        sources = (mask * state).astype(jnp.bfloat16)

        def add_term(total, item):
            rate, src, tgt, left_id, right_id = item
            prod = term_product(sources[src], left_factors[left_id], right_factors[right_id])
            old = lax.dynamic_index_in_dim(total, tgt, 0, keepdims=False)
            total = lax.dynamic_update_index_in_dim(total, old + rate * prod, tgt, 0)
            return total, None

        partial_value, unused = lax.scan(add_term, jnp.zeros(guess.shape, jnp.float32), flat)
        state = (right_side + partial_value) / diagonal
    return state
```

```python
import jax
import jax.numpy as jnp
from jax import lax
from jax.experimental import pallas as pl
from jax.experimental.pallas import tpu as pltpu
from jax.sharding import PartitionSpec as P

MESH = pl.DeviceIdType.MESH
BF = jnp.bfloat16
F32 = jnp.float32
RING = 4
CHUNKS = 4
UNROLL = 8
FAR, NEAR_B, NEAR_A = 0, 1, 2


def kernel(
    rows_hbm,
    guess_hbm,
    b_hbm,
    d_hbm,
    rate_hbm,
    source_hbm,
    target_hbm,
    lid_hbm,
    rid_hbm,
    lefts_hbm,
    rights_hbm,
    out_ref,
    gath,
    inner,
    acc,
    part,
    cross,
    send_a,
    recv_a,
    recv_b,
    mid,
    keep,
    lefts,
    rights,
    guess_ref,
    b_ref,
    d_ref,
    target_ref,
    list_ref,
    rows_s,
    rate_s,
    source_s,
    lid_s,
    rid_s,
    list_s,
    load_sem,
    ag_send,
    ag_recv,
    x_send,
    x_recv,
    a_send,
    a_recv,
    b_send,
    b_recv,
):
    depth = gath.shape[1]
    space = guess_ref.shape[0]
    terms = acc.shape[0] - 1
    targets = 2 * RING * RING
    factors = rights.shape[0]
    crow = space // CHUNKS
    hrow = crow // 2
    hops = depth // 2

    z = lax.axis_index("row")
    col = lax.axis_index("col")
    core = lax.rem(col, 2)
    xi = lax.rem(lax.div(col, 2), RING)
    yi = lax.div(col, 2 * RING)

    def at_col(y, x, c):
        return (y * RING + x) * 2 + c

    def mod(v, n):
        return lax.rem(v + n, n)

    up = {"row": mod(z + 1, depth), "col": col}
    down = {"row": mod(z - 1, depth), "col": col}
    ys = [{"row": z, "col": at_col(mod(yi + d, RING), xi, core)} for d in range(RING)]
    xs = [{"row": z, "col": at_col(yi, mod(xi + d, RING), core)} for d in range(RING)]
    sibling = {"row": z, "col": at_col(yi, xi, 1 - core)}
    peers = (up, down, sibling, *ys[1:], *xs[1:])

    def load(i, src, dst):
        copy = pltpu.make_async_copy(src, dst, load_sem.at[i])
        copy.start()
        return copy

    start_loads = [load(0, rows_hbm, rows_s), load(1, guess_hbm.at[0], guess_ref)]
    right_load = load(2, rights_hbm, rights)
    target_load = load(3, target_hbm, target_ref)
    late_loads = [
        load(4, lefts_hbm, lefts),
        load(5, b_hbm.at[0], b_ref),
        load(6, d_hbm.at[0], d_ref),
        load(7, rate_hbm, rate_s),
        load(8, source_hbm, source_s),
        load(9, lid_hbm, lid_s),
        load(10, rid_hbm, rid_s),
    ]

    barrier = pltpu.get_barrier_semaphore()
    for peer in peers:
        pl.semaphore_signal(barrier, inc=1, device_id=peer, device_id_type=MESH)
    for copy in start_loads:
        copy.wait()

    live = rows_s[0]

    def masked(value, start):
        row = lax.broadcasted_iota(jnp.int32, value.shape, 0) + start
        return jnp.where(row < live, value, 0.0).astype(BF)

    gath[0, z] = masked(guess_ref[...], 0)
    pl.semaphore_wait(barrier, len(peers))

    pending = []

    def send(src, dst, s_sem, r_sem, dev):
        copy = pltpu.make_async_remote_copy(
            src_ref=src,
            dst_ref=dst,
            send_sem=s_sem,
            recv_sem=r_sem,
            device_id=dev,
            device_id_type=MESH,
        )
        copy.start()
        pending.append(copy)
        return copy

    ag = {}

    def ag_hop(step, c, hop):
        for way, dev in ((0, up), (1, down)):
            if hop > 1:
                ag[step, c, hop - 1, way].wait_recv()
            if hop == hops and c % 2 != way:
                continue
            slot = mod(z - hop + 1, depth) if way == 0 else mod(z + hop - 1, depth)
            piece = gath.at[step, slot, pl.ds(c * crow, crow), :]
            ag[step, c, hop, way] = send(
                piece,
                piece,
                ag_send.at[step, c, hop - 1, way],
                ag_recv.at[step, c, hop - 1, way],
                dev,
            )

    def ag_end(step, c):
        ag[step, c, hops, c % 2].wait_recv()

    def products(step, hop):
        def one(i, carry):
            slot = mod(z - hop + 2 * hop * i, depth)
            for r in range(factors):
                inner[slot, r] = lax.dot_general(
                    gath[step, slot],
                    rights[r],
                    (((1,), (1,)), ((), ())),
                    preferred_element_type=F32,
                ).astype(BF)
            return carry

        lax.fori_loop(0, 2 if 0 < hop < hops else 1, one, 0)

    def make_lists():
        tgt = jnp.broadcast_to(target_ref[...], (terms, terms))
        ii = lax.broadcasted_iota(jnp.int32, (terms, terms), 0)
        jj = lax.broadcasted_iota(jnp.int32, (terms, terms), 1)
        column = jnp.max(jnp.where(ii == jj, tgt, 0), axis=1, keepdims=True)
        same = (column == tgt) & (ii < jj)
        prev = jnp.max(jnp.where(same, ii + 1, 0), axis=0, keepdims=True)
        list_ref[0:1, 0:terms] = prev
        qi = lax.broadcasted_iota(jnp.int32, (terms, targets), 0)
        qj = lax.broadcasted_iota(jnp.int32, (terms, targets), 1)
        last = jnp.max(jnp.where(column == qj, qi + 1, 0), axis=0, keepdims=True)
        list_ref[1:2, 0:targets] = last
        copy = pltpu.make_async_copy(list_ref, list_s, load_sem.at[11])
        copy.start()
        return copy

    def sums(p):
        rows = pl.ds(p * 2 * crow, 2 * crow)

        def one(t, carry):
            value = jnp.dot(
                lefts[lid_s[0, t], rows, :],
                inner[source_s[0, t], rid_s[0, t]],
                preferred_element_type=F32,
            )
            acc[t + 1, rows, :] = value * rate_s[0, t] + acc[list_s[0, t], rows, :]
            return carry

        lax.fori_loop(0, terms, one, 0, unroll=UNROLL)

    class Reduce:
        def __init__(self, step, finish):
            self.step, self.finish = step, finish
            self.crossing, self.a, self.b = {}, {}, {}

        def axes(self, c):
            return (yi, ys, xi, xs) if c % 2 == 0 else (xi, xs, yi, ys)

        def own(self, c, d, k, half):
            y, x = (d, k) if c % 2 == 0 else (k, d)
            spot = list_s[1, at_col(y, x, core)]
            rows = pl.ds(c * crow + half * hrow, hrow)
            other = cross[self.step, c, y, x, pl.ds(half * hrow, hrow), :]
            return acc[spot, rows, :] + other.astype(F32)

        def cross(self, c):
            rows = pl.ds(c * crow, crow)

            def one(k, carry):
                y, x = lax.div(k, RING), lax.rem(k, RING)
                part[y, x, rows, :] = acc[list_s[1, at_col(y, x, 1 - core)], rows, :].astype(BF)
                return carry

            lax.fori_loop(0, RING * RING, one, 0, unroll=RING)
            self.crossing[c] = send(
                part.at[:, :, rows, :],
                cross.at[self.step, c],
                x_send.at[self.step, c],
                x_recv.at[self.step, c],
                sibling,
            )

        def go(self, c, way, kind, d, half, extra=None):
            me, devs, _, _ = self.axes(c)
            dest = mod(me + d, RING)
            for k in range(RING):
                value = self.own(c, dest, k, half)
                if extra is not None:
                    value = value + extra[k].astype(F32)
                send_a[c, way, kind, k] = value.astype(BF)
            self.a[c, way, kind] = send(
                send_a.at[c, way, kind],
                recv_a.at[self.step, c, way, kind],
                a_send.at[self.step, c, way, kind],
                a_recv.at[self.step, c, way, kind],
                devs[1 if way == 0 else RING - 1],
            )

        def far(self, c):
            self.crossing[c].wait_recv()
            self.go(c, 0, FAR, 2, 0)
            self.go(c, 1, FAR, 2, 1)

        def near_b(self, c):
            self.go(c, 0, NEAR_B, 1, 1)
            self.go(c, 1, NEAR_B, -1, 0)

        def near_a(self, c):
            for way, d, half in ((0, 1, 0), (1, -1, 1)):
                self.a[c, way, FAR].wait_recv()
                self.go(c, way, NEAR_A, d, half, recv_a.at[self.step, c, way, FAR])

        def middle(self, c):
            me, _, bme, bdevs = self.axes(c)
            for kind in (NEAR_B, NEAR_A):
                for way in (0, 1):
                    self.a[c, way, kind].wait_recv()
            for d in (2, 1, 3, 0):
                k = mod(bme + d, RING)
                for half, kinds in ((0, (NEAR_A, NEAR_B)), (1, (NEAR_B, NEAR_A))):
                    rows = slice(half * hrow, half * hrow + hrow)
                    total = self.own(c, me, k, half)
                    for way in (0, 1):
                        total = total + recv_a[self.step, c, way, kinds[way], k].astype(F32)
                    if d == 0:
                        keep[c, rows, :] = total
                    else:
                        mid[c, d - 1, rows, :] = total.astype(BF)
                if d > 0:
                    self.b[c, d] = send(
                        mid.at[c, d - 1],
                        recv_b.at[self.step, c, d - 1],
                        b_send.at[self.step, c, d - 1],
                        b_recv.at[self.step, c, d - 1],
                        bdevs[d],
                    )

        def end(self, c):
            total = keep[c]
            for d in (1, 3, 2):
                self.b[c, d].wait_recv()
                total = total + recv_b[self.step, c, d - 1].astype(F32)
            rows = slice(c * crow, c * crow + crow)
            self.finish(c, rows, (b_ref[rows, :] + total) / d_ref[rows, :])

    def both(call, p):
        call(2 * p)
        call(2 * p + 1)

    for c in range(CHUNKS):
        ag_hop(0, c, 1)
    target_load.wait()
    lists = make_lists()
    right_load.wait()
    products(0, 0)
    for hop in range(2, hops + 1):
        for c in range(CHUNKS):
            ag_hop(0, c, hop)
        products(0, hop - 1)
    for c in range(CHUNKS):
        ag_end(0, c)
    products(0, hops)
    acc[0] = jnp.zeros_like(acc[0])
    lists.wait()
    for copy in late_loads:
        copy.wait()

    def reduce(step, finish, hook):
        red = Reduce(step, finish)
        sums(0)
        both(red.cross, 0)
        sums(1)
        both(red.cross, 1)
        both(red.far, 0)
        both(red.near_b, 0)
        both(red.far, 1)
        both(red.near_a, 0)
        both(red.near_b, 1)
        both(red.near_a, 1)
        both(red.middle, 0)
        both(red.middle, 1)
        both(red.end, 0)
        hook(0)
        both(red.end, 1)
        hook(1)

    def finish0(c, rows, value):
        gath[1, z, rows, :] = masked(value, rows.start)

    def hook0(p):
        both(lambda c: ag_hop(1, c, 1), p)

    reduce(0, finish0, hook0)
    products(1, 0)
    for hop in range(2, hops + 1):
        for c in range(CHUNKS):
            ag_hop(1, c, hop)
        products(1, hop - 1)
    for c in range(CHUNKS):
        ag_end(1, c)
    products(1, hops)
    for copy in pending:
        copy.wait_send()
    pending.clear()

    def finish1(c, rows, value):
        out_ref[rows, :] = value

    reduce(1, finish1, lambda p: None)
    for copy in pending:
        copy.wait_send()


def body(
    slab_rows,
    guess,
    right_side,
    diagonal,
    rates,
    term_source,
    term_target,
    term_left,
    term_right,
    left_factors,
    right_factors,
):
    space = guess.shape[1]
    depth = lax.axis_size("row")
    factors = left_factors.shape[0]
    terms = rates.shape[1]
    crow = space // CHUNKS
    hrow = crow // 2
    vmem = pl.BlockSpec(memory_space=pltpu.VMEM)
    hbm = pl.BlockSpec(memory_space=pl.ANY)
    dma = pltpu.SemaphoreType.DMA
    hops = depth // 2
    args = (
        slab_rows,
        guess,
        right_side,
        diagonal,
        rates,
        term_source,
        term_target,
        term_left,
        term_right,
        left_factors,
        right_factors,
    )
    out = pl.pallas_call(
        kernel,
        out_shape=jax.ShapeDtypeStruct((space, space), F32),
        in_specs=[hbm] * len(args),
        out_specs=vmem,
        scratch_shapes=[
            pltpu.VMEM((2, depth, space, space), BF),
            pltpu.VMEM((depth, factors, space, space), BF),
            pltpu.VMEM((terms + 1, space, space), F32),
            pltpu.VMEM((RING, RING, space, space), BF),
            pltpu.VMEM((2, CHUNKS, RING, RING, crow, space), BF),
            pltpu.VMEM((CHUNKS, 2, 3, RING, hrow, space), BF),
            pltpu.VMEM((2, CHUNKS, 2, 3, RING, hrow, space), BF),
            pltpu.VMEM((2, CHUNKS, RING - 1, crow, space), BF),
            pltpu.VMEM((CHUNKS, RING - 1, crow, space), BF),
            pltpu.VMEM((CHUNKS, crow, space), F32),
            pltpu.VMEM((factors, space, space), BF),
            pltpu.VMEM((factors, space, space), BF),
            pltpu.VMEM((space, space), F32),
            pltpu.VMEM((space, space), F32),
            pltpu.VMEM((space, space), F32),
            pltpu.VMEM((1, terms), jnp.int32),
            pltpu.VMEM((8, 128), jnp.int32),
            pltpu.SMEM((1,), jnp.int32),
            pltpu.SMEM((1, terms), F32),
            pltpu.SMEM((1, terms), jnp.int32),
            pltpu.SMEM((1, terms), jnp.int32),
            pltpu.SMEM((1, terms), jnp.int32),
            pltpu.SMEM((8, 128), jnp.int32),
            dma((12,)),
            dma((2, CHUNKS, hops, 2)),
            dma((2, CHUNKS, hops, 2)),
            dma((2, CHUNKS)),
            dma((2, CHUNKS)),
            dma((2, CHUNKS, 2, 3)),
            dma((2, CHUNKS, 2, 3)),
            dma((2, CHUNKS, RING - 1)),
            dma((2, CHUNKS, RING - 1)),
        ],
        compiler_params=pltpu.CompilerParams(
            collective_id=0, has_side_effects=True, vmem_limit_bytes=60 * 1024 * 1024
        ),
        cost_estimate=pl.CostEstimate(
            flops=4 * (depth * factors + terms) * space**3,
            bytes_accessed=4 * 1024 * 1024,
            transcendentals=0,
        ),
    )(*args)
    return out.reshape(1, space, space)


def solution(mesh):
    in_specs = (
        P(("row", "col")),
        P(("row", "col"), None, None),
        P(("row", "col"), None, None),
        P(("row", "col"), None, None),
        P("row", "col"),
        P("row", "col"),
        P("row", "col"),
        P("row", "col"),
        P("row", "col"),
        P(),
        P(),
    )
    out_specs = P(("row", "col"), None, None)
    return jax.shard_map(body, mesh=mesh, in_specs=in_specs, out_specs=out_specs, check_vma=False)
```

```python
import jax
import jax.numpy as jnp
from jax import lax
from jax.experimental import pallas as pl
from jax.experimental.pallas import tpu as pltpu
from jax.sharding import PartitionSpec as P

MESH = pl.DeviceIdType.MESH
BF = jnp.bfloat16
F32 = jnp.float32
RING = 4
CHUNKS = 4
UNROLL = 12
PARTS = 3
FAR, NEAR_B, NEAR_A = 0, 1, 2


def kernel(
    rows_hbm,
    guess_hbm,
    b_hbm,
    d_hbm,
    rate_hbm,
    source_hbm,
    target_hbm,
    lid_hbm,
    rid_hbm,
    lefts_hbm,
    rights_hbm,
    out_ref,
    gath,
    inner,
    acc,
    part,
    cross,
    send_a,
    recv_a,
    recv_b,
    mid,
    keep,
    lefts,
    rights,
    guess_ref,
    b_ref,
    d_ref,
    target_ref,
    list_ref,
    rows_s,
    rate_s,
    source_s,
    lid_s,
    rid_s,
    list_s,
    load_sem,
    ag_send,
    ag_recv,
    x_send,
    x_recv,
    a_send,
    a_recv,
    b_send,
    b_recv,
):
    depth = gath.shape[1]
    space = guess_ref.shape[0]
    terms = acc.shape[0] - 1
    targets = 2 * RING * RING
    factors = rights.shape[0]
    crow = space // CHUNKS
    hrow = crow // 2
    hops = depth // 2

    z = lax.axis_index("row")
    col = lax.axis_index("col")
    core = lax.rem(col, 2)
    xi = lax.rem(lax.div(col, 2), RING)
    yi = lax.div(col, 2 * RING)

    def at_col(y, x, c):
        return (y * RING + x) * 2 + c

    def mod(v, n):
        return lax.rem(v + n, n)

    up = {"row": mod(z + 1, depth), "col": col}
    down = {"row": mod(z - 1, depth), "col": col}
    ys = [{"row": z, "col": at_col(mod(yi + d, RING), xi, core)} for d in range(RING)]
    xs = [{"row": z, "col": at_col(yi, mod(xi + d, RING), core)} for d in range(RING)]
    sibling = {"row": z, "col": at_col(yi, xi, 1 - core)}
    peers = (up, down, sibling, *ys[1:], *xs[1:])

    def load(i, src, dst):
        copy = pltpu.make_async_copy(src, dst, load_sem.at[i])
        copy.start()
        return copy

    start_loads = [load(0, rows_hbm, rows_s), load(1, guess_hbm.at[0], guess_ref)]
    right_load = load(2, rights_hbm, rights)
    target_load = load(3, target_hbm, target_ref)
    late_loads = [
        load(4, lefts_hbm, lefts),
        load(5, b_hbm.at[0], b_ref),
        load(6, d_hbm.at[0], d_ref),
        load(7, rate_hbm, rate_s),
        load(8, source_hbm, source_s),
        load(9, lid_hbm, lid_s),
        load(10, rid_hbm, rid_s),
    ]

    barrier = pltpu.get_barrier_semaphore()
    for peer in peers:
        pl.semaphore_signal(barrier, inc=1, device_id=peer, device_id_type=MESH)
    for copy in start_loads:
        copy.wait()

    live = rows_s[0]

    def masked(value, start):
        row = lax.broadcasted_iota(jnp.int32, value.shape, 0) + start
        return jnp.where(row < live, value, 0.0).astype(BF)

    gath[0, z] = masked(guess_ref[...], 0)
    pl.semaphore_wait(barrier, len(peers))

    pending = []

    def send(src, dst, s_sem, r_sem, dev):
        copy = pltpu.make_async_remote_copy(
            src_ref=src,
            dst_ref=dst,
            send_sem=s_sem,
            recv_sem=r_sem,
            device_id=dev,
            device_id_type=MESH,
        )
        copy.start()
        pending.append(copy)
        return copy

    ag = {}

    def ag_hop(step, c, hop):
        for way, dev in ((0, up), (1, down)):
            if hop > 1:
                ag[step, c, hop - 1, way].wait_recv()
            if hop == hops and c % 2 != way:
                continue
            slot = mod(z - hop + 1, depth) if way == 0 else mod(z + hop - 1, depth)
            piece = gath.at[step, slot, pl.ds(c * crow, crow), :]
            ag[step, c, hop, way] = send(
                piece,
                piece,
                ag_send.at[step, c, hop - 1, way],
                ag_recv.at[step, c, hop - 1, way],
                dev,
            )

    def ag_end(step, c):
        ag[step, c, hops, c % 2].wait_recv()

    def products(step, offset):
        slot = mod(z + offset, depth)
        for r in range(factors):
            inner[slot, r] = lax.dot_general(
                gath[step, slot],
                rights[r],
                (((1,), (1,)), ((), ())),
                preferred_element_type=F32,
            ).astype(BF)

    def ag_rest(step):
        for hop in range(2, hops + 1):
            for c in range(CHUNKS):
                ag_hop(step, c, hop)
                if c == 1 and hop > 2:
                    products(step, hop - 2)
                if c == CHUNKS - 1:
                    products(step, 1 - hop)
        ag_end(step, 0)
        ag_end(step, 1)
        products(step, hops - 1)
        ag_end(step, 2)
        ag_end(step, 3)
        products(step, hops)

    def make_lists():
        tgt = jnp.broadcast_to(target_ref[...], (terms, terms))
        ii = lax.broadcasted_iota(jnp.int32, (terms, terms), 0)
        jj = lax.broadcasted_iota(jnp.int32, (terms, terms), 1)
        column = jnp.max(jnp.where(ii == jj, tgt, 0), axis=1, keepdims=True)
        same = (column == tgt) & (ii < jj)
        prev = jnp.max(jnp.where(same, ii + 1, 0), axis=0, keepdims=True)
        list_ref[0:1, 0:terms] = prev
        qi = lax.broadcasted_iota(jnp.int32, (terms, targets), 0)
        qj = lax.broadcasted_iota(jnp.int32, (terms, targets), 1)
        last = jnp.max(jnp.where(column == qj, qi + 1, 0), axis=0, keepdims=True)
        list_ref[1:2, 0:targets] = last
        copy = pltpu.make_async_copy(list_ref, list_s, load_sem.at[11])
        copy.start()
        return copy

    def sums(p, part, parts):
        rows = pl.ds(p * 2 * crow, 2 * crow)

        def one(t, carry):
            value = jnp.dot(
                lefts[lid_s[0, t], rows, :],
                inner[source_s[0, t], rid_s[0, t]],
                preferred_element_type=F32,
            )
            acc[t + 1, rows, :] = value * rate_s[0, t] + acc[list_s[0, t], rows, :]
            return carry

        size = terms // PARTS
        lax.fori_loop(part * size, parts * size, one, 0, unroll=UNROLL)

    class Reduce:
        def __init__(self, step, finish):
            self.step, self.finish = step, finish
            self.crossing, self.a, self.b = {}, {}, {}

        def axes(self, c):
            return (yi, ys, xi, xs) if c % 2 == 0 else (xi, xs, yi, ys)

        def spot(self, c, d, k, side):
            me = self.axes(c)[0]
            dest = mod(me + d, RING)
            y, x = (dest, k) if c % 2 == 0 else (k, dest)
            return list_s[1, at_col(y, x, side)]

        def own(self, c, d, k, half):
            rows = pl.ds(c * crow + half * hrow, hrow)
            other = cross[self.step, c, d % RING, k, pl.ds(half * hrow, hrow), :]
            return acc[self.spot(c, d, k, core), rows, :] + other.astype(F32)

        def cross(self, c, d):
            rows = pl.ds(c * crow, crow)
            for k in range(RING):
                part[c, d, k] = acc[self.spot(c, d, k, 1 - core), rows, :].astype(BF)
            self.crossing[c, d] = send(
                part.at[c, d],
                cross.at[self.step, c, d],
                x_send.at[self.step, c, d],
                x_recv.at[self.step, c, d],
                sibling,
            )

        def go(self, c, way, kind, d, half, extra=None):
            devs = self.axes(c)[1]
            for k in range(RING):
                value = self.own(c, d, k, half)
                if extra is not None:
                    value = value + extra[k].astype(F32)
                send_a[c, way, kind, k] = value.astype(BF)
            self.a[c, way, kind] = send(
                send_a.at[c, way, kind],
                recv_a.at[self.step, c, way, kind],
                a_send.at[self.step, c, way, kind],
                a_recv.at[self.step, c, way, kind],
                devs[1 if way == 0 else RING - 1],
            )

        def far(self, c):
            self.crossing[c, 2].wait_recv()
            self.go(c, 0, FAR, 2, 0)
            self.go(c, 1, FAR, 2, 1)

        def near_b(self, c):
            self.crossing[c, 1].wait_recv()
            self.go(c, 0, NEAR_B, 1, 1)
            self.crossing[c, 3].wait_recv()
            self.go(c, 1, NEAR_B, 3, 0)

        def near_a(self, c):
            for way, d, half in ((0, 1, 0), (1, 3, 1)):
                self.a[c, way, FAR].wait_recv()
                self.go(c, way, NEAR_A, d, half, recv_a.at[self.step, c, way, FAR])

        def middle(self, c):
            _, _, bme, bdevs = self.axes(c)
            self.crossing[c, 0].wait_recv()
            for kind in (NEAR_B, NEAR_A):
                for way in (0, 1):
                    self.a[c, way, kind].wait_recv()
            for d in (2, 1, 3, 0):
                k = mod(bme + d, RING)
                for half, kinds in ((0, (NEAR_A, NEAR_B)), (1, (NEAR_B, NEAR_A))):
                    rows = slice(half * hrow, half * hrow + hrow)
                    total = self.own(c, 0, k, half)
                    for way in (0, 1):
                        total = total + recv_a[self.step, c, way, kinds[way], k].astype(F32)
                    if d == 0:
                        keep[c, rows, :] = total
                    else:
                        mid[c, d - 1, rows, :] = total.astype(BF)
                if d > 0:
                    self.b[c, d] = send(
                        mid.at[c, d - 1],
                        recv_b.at[self.step, c, d - 1],
                        b_send.at[self.step, c, d - 1],
                        b_recv.at[self.step, c, d - 1],
                        bdevs[d],
                    )

        def end(self, c):
            total = keep[c]
            for d in (1, 3, 2):
                self.b[c, d].wait_recv()
                total = total + recv_b[self.step, c, d - 1].astype(F32)
            rows = slice(c * crow, c * crow + crow)
            self.finish(c, rows, (b_ref[rows, :] + total) / d_ref[rows, :])

    def both(call, p):
        call(2 * p)
        call(2 * p + 1)

    for c in range(CHUNKS):
        ag_hop(0, c, 1)
    target_load.wait()
    lists = make_lists()
    right_load.wait()
    products(0, 0)
    acc[0] = jnp.zeros_like(acc[0])
    ag_rest(0)
    lists.wait()
    for copy in late_loads:
        copy.wait()

    def reduce(step, finish, hook):
        red = Reduce(step, finish)

        def spread(p):
            for d in (2, 1, 3, 0):
                both(lambda c: red.cross(c, d), p)

        sums(0, 0, 3)
        spread(0)
        sums(1, 0, 1)
        both(red.far, 0)
        sums(1, 1, 2)
        both(red.near_b, 0)
        sums(1, 2, 3)
        spread(1)
        both(red.far, 1)
        both(red.near_a, 0)
        both(red.near_b, 1)
        both(red.near_a, 1)
        both(red.middle, 0)
        both(red.middle, 1)
        both(red.end, 0)
        hook(0)
        both(red.end, 1)
        hook(1)

    def finish0(c, rows, value):
        gath[1, z, rows, :] = masked(value, rows.start)

    def hook0(p):
        both(lambda c: ag_hop(1, c, 1), p)

    reduce(0, finish0, hook0)
    products(1, 0)
    ag_rest(1)
    for copy in pending:
        copy.wait_send()
    pending.clear()

    def finish1(c, rows, value):
        out_ref[rows, :] = value

    reduce(1, finish1, lambda p: None)
    for copy in pending:
        copy.wait_send()


def body(
    slab_rows,
    guess,
    right_side,
    diagonal,
    rates,
    term_source,
    term_target,
    term_left,
    term_right,
    left_factors,
    right_factors,
):
    space = guess.shape[1]
    depth = lax.axis_size("row")
    factors = left_factors.shape[0]
    terms = rates.shape[1]
    crow = space // CHUNKS
    hrow = crow // 2
    vmem = pl.BlockSpec(memory_space=pltpu.VMEM)
    hbm = pl.BlockSpec(memory_space=pl.ANY)
    dma = pltpu.SemaphoreType.DMA
    hops = depth // 2
    args = (
        slab_rows,
        guess,
        right_side,
        diagonal,
        rates,
        term_source,
        term_target,
        term_left,
        term_right,
        left_factors,
        right_factors,
    )
    out = pl.pallas_call(
        kernel,
        out_shape=pltpu.VMEM((space, space), F32),
        in_specs=[hbm] * len(args),
        out_specs=vmem,
        scratch_shapes=[
            pltpu.VMEM((2, depth, space, space), BF),
            pltpu.VMEM((depth, factors, space, space), BF),
            pltpu.VMEM((terms + 1, space, space), F32),
            pltpu.VMEM((CHUNKS, RING, RING, crow, space), BF),
            pltpu.VMEM((2, CHUNKS, RING, RING, crow, space), BF),
            pltpu.VMEM((CHUNKS, 2, 3, RING, hrow, space), BF),
            pltpu.VMEM((2, CHUNKS, 2, 3, RING, hrow, space), BF),
            pltpu.VMEM((2, CHUNKS, RING - 1, crow, space), BF),
            pltpu.VMEM((CHUNKS, RING - 1, crow, space), BF),
            pltpu.VMEM((CHUNKS, crow, space), F32),
            pltpu.VMEM((factors, space, space), BF),
            pltpu.VMEM((factors, space, space), BF),
            pltpu.VMEM((space, space), F32),
            pltpu.VMEM((space, space), F32),
            pltpu.VMEM((space, space), F32),
            pltpu.VMEM((1, terms), jnp.int32),
            pltpu.VMEM((8, 128), jnp.int32),
            pltpu.SMEM((1,), jnp.int32),
            pltpu.SMEM((1, terms), F32),
            pltpu.SMEM((1, terms), jnp.int32),
            pltpu.SMEM((1, terms), jnp.int32),
            pltpu.SMEM((1, terms), jnp.int32),
            pltpu.SMEM((8, 128), jnp.int32),
            dma((12,)),
            dma((2, CHUNKS, hops, 2)),
            dma((2, CHUNKS, hops, 2)),
            dma((2, CHUNKS, RING)),
            dma((2, CHUNKS, RING)),
            dma((2, CHUNKS, 2, 3)),
            dma((2, CHUNKS, 2, 3)),
            dma((2, CHUNKS, RING - 1)),
            dma((2, CHUNKS, RING - 1)),
        ],
        compiler_params=pltpu.CompilerParams(
            collective_id=0, has_side_effects=True, vmem_limit_bytes=60 * 1024 * 1024
        ),
        cost_estimate=pl.CostEstimate(
            flops=4 * (depth * factors + terms) * space**3,
            bytes_accessed=4 * 1024 * 1024,
            transcendentals=0,
        ),
    )(*args)
    return out.reshape(1, space, space)


def solution(mesh):
    in_specs = (
        P(("row", "col")),
        P(("row", "col"), None, None),
        P(("row", "col"), None, None),
        P(("row", "col"), None, None),
        P("row", "col"),
        P("row", "col"),
        P("row", "col"),
        P("row", "col"),
        P("row", "col"),
        P(),
        P(),
    )
    out_specs = P(("row", "col"), None, None)
    return jax.shard_map(body, mesh=mesh, in_specs=in_specs, out_specs=out_specs, check_vma=False)
```

```python
import jax
import jax.numpy as jnp
from jax import lax
from jax.experimental import pallas as pl
from jax.experimental.pallas import tpu as pltpu
from jax.sharding import PartitionSpec as P

MESH = pl.DeviceIdType.MESH
BF = jnp.bfloat16
F32 = jnp.float32
RING = 4
CHUNKS = 4
UNROLL = 12
PARTS = 3
FAR, NEAR_B, NEAR_A = 0, 1, 2


def kernel(
    rows_hbm,
    guess_hbm,
    b_hbm,
    d_hbm,
    rate_hbm,
    source_hbm,
    target_hbm,
    lid_hbm,
    rid_hbm,
    lefts_hbm,
    rights_hbm,
    out_ref,
    gath,
    inner,
    acc,
    part,
    cross,
    send_a,
    recv_a,
    recv_b,
    mid,
    keep,
    lefts,
    rights,
    guess_ref,
    b_ref,
    d_ref,
    target_ref,
    list_ref,
    rows_s,
    rate_s,
    source_s,
    lid_s,
    rid_s,
    list_s,
    load_sem,
    ag_send,
    ag_recv,
    x_send,
    x_recv,
    a_send,
    a_recv,
    b_send,
    b_recv,
):
    depth = gath.shape[1]
    space = guess_ref.shape[0]
    terms = acc.shape[0] - 1
    targets = 2 * RING * RING
    factors = rights.shape[0]
    crow = space // CHUNKS
    hrow = crow // 2
    hops = depth // 2

    z = lax.axis_index("row")
    col = lax.axis_index("col")
    core = lax.rem(col, 2)
    xi = lax.rem(lax.div(col, 2), RING)
    yi = lax.div(col, 2 * RING)

    def at_col(y, x, c):
        return (y * RING + x) * 2 + c

    def mod(v, n):
        return lax.rem(v + n, n)

    up = {"row": mod(z + 1, depth), "col": col}
    down = {"row": mod(z - 1, depth), "col": col}
    ys = [{"row": z, "col": at_col(mod(yi + d, RING), xi, core)} for d in range(RING)]
    xs = [{"row": z, "col": at_col(yi, mod(xi + d, RING), core)} for d in range(RING)]
    sibling = {"row": z, "col": at_col(yi, xi, 1 - core)}
    peers = (up, down, sibling, *ys[1:], *xs[1:])

    def load(i, src, dst):
        copy = pltpu.make_async_copy(src, dst, load_sem.at[i])
        copy.start()
        return copy

    barrier = pltpu.get_barrier_semaphore()
    for peer in peers:
        pl.semaphore_signal(barrier, inc=1, device_id=peer, device_id_type=MESH)
    start_loads = [load(0, rows_hbm, rows_s), load(1, guess_hbm.at[0], guess_ref)]
    for copy in start_loads:
        copy.wait()

    live = rows_s[0]

    def masked(value, start):
        row = lax.broadcasted_iota(jnp.int32, value.shape, 0) + start
        return jnp.where(row < live, value, 0.0).astype(BF)

    gath[0, z] = masked(guess_ref[...], 0)
    pl.semaphore_wait(barrier, len(peers))

    pending = []

    def send(src, dst, s_sem, r_sem, dev):
        copy = pltpu.make_async_remote_copy(
            src_ref=src,
            dst_ref=dst,
            send_sem=s_sem,
            recv_sem=r_sem,
            device_id=dev,
            device_id_type=MESH,
        )
        copy.start()
        pending.append(copy)
        return copy

    def drain(left):
        while len(pending) > left:
            pending.pop(0).wait_send()

    ag = {}

    def ag_hop(step, c, hop):
        for way, dev in ((0, up), (1, down)):
            if hop > 1:
                ag[step, c, hop - 1, way].wait_recv()
            if hop == hops and c % 2 != way:
                continue
            slot = mod(z - hop + 1, depth) if way == 0 else mod(z + hop - 1, depth)
            piece = gath.at[step, slot, pl.ds(c * crow, crow), :]
            ag[step, c, hop, way] = send(
                piece,
                piece,
                ag_send.at[step, c, hop - 1, way],
                ag_recv.at[step, c, hop - 1, way],
                dev,
            )

    def ag_end(step, c):
        ag[step, c, hops, c % 2].wait_recv()

    def products(step, offset):
        slot = mod(z + offset, depth)
        for r in range(factors):
            inner[slot, r] = lax.dot_general(
                gath[step, slot],
                rights[r],
                (((1,), (1,)), ((), ())),
                preferred_element_type=F32,
            ).astype(BF)

    def ag_rest(step):
        for hop in range(2, hops + 1):
            for c in range(CHUNKS):
                if step == 1:
                    drain(16)
                ag_hop(step, c, hop)
                if c == 1 and hop > 2:
                    products(step, hop - 2)
                if c == CHUNKS - 1:
                    products(step, 1 - hop)
        ag_end(step, 0)
        ag_end(step, 1)
        products(step, hops - 1)
        ag_end(step, 2)
        ag_end(step, 3)
        products(step, hops)

    def make_lists():
        tgt = jnp.broadcast_to(target_ref[...], (terms, terms))
        ii = lax.broadcasted_iota(jnp.int32, (terms, terms), 0)
        jj = lax.broadcasted_iota(jnp.int32, (terms, terms), 1)
        column = jnp.max(jnp.where(ii == jj, tgt, 0), axis=1, keepdims=True)
        same = (column == tgt) & (ii < jj)
        prev = jnp.max(jnp.where(same, ii + 1, 0), axis=0, keepdims=True)
        list_ref[0:1, 0:terms] = prev
        qi = lax.broadcasted_iota(jnp.int32, (terms, targets), 0)
        qj = lax.broadcasted_iota(jnp.int32, (terms, targets), 1)
        last = jnp.max(jnp.where(column == qj, qi + 1, 0), axis=0, keepdims=True)
        list_ref[1:2, 0:targets] = last
        copy = pltpu.make_async_copy(list_ref, list_s, load_sem.at[11])
        copy.start()
        return copy

    def sums(p, part, parts):
        rows = pl.ds(p * 2 * crow, 2 * crow)

        def one(t, carry):
            value = jnp.dot(
                lefts[lid_s[0, t], rows, :],
                inner[source_s[0, t], rid_s[0, t]],
                preferred_element_type=F32,
            )
            acc[t + 1, rows, :] = value * rate_s[0, t] + acc[list_s[0, t], rows, :]
            return carry

        size = terms // PARTS
        lax.fori_loop(part * size, parts * size, one, 0, unroll=UNROLL)

    class Reduce:
        def __init__(self, step, finish):
            self.step, self.finish = step, finish
            self.crossing, self.a, self.b = {}, {}, {}

        def axes(self, c):
            return (yi, ys, xi, xs) if c % 2 == 0 else (xi, xs, yi, ys)

        def spot(self, c, d, k, side):
            me = self.axes(c)[0]
            dest = mod(me + d, RING)
            y, x = (dest, k) if c % 2 == 0 else (k, dest)
            return list_s[1, at_col(y, x, side)]

        def own(self, c, d, k, half):
            rows = pl.ds(c * crow + half * hrow, hrow)
            other = cross[self.step, c, d % RING, k, pl.ds(half * hrow, hrow), :]
            return acc[self.spot(c, d, k, core), rows, :] + other.astype(F32)

        def cross(self, c, d):
            rows = pl.ds(c * crow, crow)
            for k in range(RING):
                part[c, d, k] = acc[self.spot(c, d, k, 1 - core), rows, :].astype(BF)
            self.crossing[c, d] = send(
                part.at[c, d],
                cross.at[self.step, c, d],
                x_send.at[self.step, c, d],
                x_recv.at[self.step, c, d],
                sibling,
            )

        def go(self, c, way, kind, d, half, extra=None):
            devs = self.axes(c)[1]
            for k in range(RING):
                value = self.own(c, d, k, half)
                if extra is not None:
                    value = value + extra[k].astype(F32)
                send_a[c, way, kind, k] = value.astype(BF)
            self.a[c, way, kind] = send(
                send_a.at[c, way, kind],
                recv_a.at[self.step, c, way, kind],
                a_send.at[self.step, c, way, kind],
                a_recv.at[self.step, c, way, kind],
                devs[1 if way == 0 else RING - 1],
            )

        def far(self, c):
            self.crossing[c, 2].wait_recv()
            self.go(c, 0, FAR, 2, 0)
            self.go(c, 1, FAR, 2, 1)

        def near_b(self, c):
            self.crossing[c, 1].wait_recv()
            self.go(c, 0, NEAR_B, 1, 1)
            self.crossing[c, 3].wait_recv()
            self.go(c, 1, NEAR_B, 3, 0)

        def near_a(self, c):
            for way, d, half in ((0, 1, 0), (1, 3, 1)):
                self.a[c, way, FAR].wait_recv()
                self.go(c, way, NEAR_A, d, half, recv_a.at[self.step, c, way, FAR])

        def middle(self, c):
            _, _, bme, bdevs = self.axes(c)
            self.crossing[c, 0].wait_recv()
            for kind in (NEAR_B, NEAR_A):
                for way in (0, 1):
                    self.a[c, way, kind].wait_recv()
            for d in (2, 1, 3, 0):
                k = mod(bme + d, RING)
                for half, kinds in ((0, (NEAR_A, NEAR_B)), (1, (NEAR_B, NEAR_A))):
                    rows = slice(half * hrow, half * hrow + hrow)
                    total = self.own(c, 0, k, half)
                    for way in (0, 1):
                        total = total + recv_a[self.step, c, way, kinds[way], k].astype(F32)
                    if d == 0:
                        keep[c, rows, :] = total
                    else:
                        mid[c, d - 1, rows, :] = total.astype(BF)
                if d > 0:
                    self.b[c, d] = send(
                        mid.at[c, d - 1],
                        recv_b.at[self.step, c, d - 1],
                        b_send.at[self.step, c, d - 1],
                        b_recv.at[self.step, c, d - 1],
                        bdevs[d],
                    )

        def end(self, c):
            total = keep[c]
            for d in (1, 3, 2):
                self.b[c, d].wait_recv()
                total = total + recv_b[self.step, c, d - 1].astype(F32)
            rows = slice(c * crow, c * crow + crow)
            self.finish(c, rows, (b_ref[rows, :] + total) / d_ref[rows, :])

    def both(call, p):
        call(2 * p)
        call(2 * p + 1)

    for c in range(CHUNKS):
        ag_hop(0, c, 1)
    right_load = load(2, rights_hbm, rights)
    target_load = load(3, target_hbm, target_ref)
    late_loads = [
        load(4, lefts_hbm, lefts),
        load(5, b_hbm.at[0], b_ref),
        load(6, d_hbm.at[0], d_ref),
        load(7, rate_hbm, rate_s),
        load(8, source_hbm, source_s),
        load(9, lid_hbm, lid_s),
        load(10, rid_hbm, rid_s),
    ]

    target_load.wait()
    lists = make_lists()
    right_load.wait()
    products(0, 0)
    acc[0] = jnp.zeros_like(acc[0])
    ag_rest(0)
    lists.wait()
    for copy in late_loads:
        copy.wait()

    def reduce(step, finish, hook):
        red = Reduce(step, finish)

        def spread(p):
            for d in (2, 1, 3, 0):
                both(lambda c: red.cross(c, d), p)

        sums(0, 0, 3)
        spread(0)
        sums(1, 0, 1)
        both(red.far, 0)
        sums(1, 1, 2)
        both(red.near_b, 0)
        sums(1, 2, 3)
        spread(1)
        both(red.far, 1)
        drain(20)
        both(red.near_a, 0)
        both(red.near_b, 1)
        both(red.near_a, 1)
        drain(20)
        both(red.middle, 0)
        both(red.middle, 1)
        for c in range(CHUNKS):
            red.end(c)
            hook(c)

    def finish0(c, rows, value):
        gath[1, z, rows, :] = masked(value, rows.start)

    def hook0(c):
        ag_hop(1, c, 1)

    reduce(0, finish0, hook0)
    products(1, 0)
    ag_rest(1)
    drain(16)

    def finish1(c, rows, value):
        out_ref[rows, :] = value

    reduce(1, finish1, lambda p: None)
    for copy in pending:
        copy.wait_send()


def body(
    slab_rows,
    guess,
    right_side,
    diagonal,
    rates,
    term_source,
    term_target,
    term_left,
    term_right,
    left_factors,
    right_factors,
):
    space = guess.shape[1]
    depth = lax.axis_size("row")
    factors = left_factors.shape[0]
    terms = rates.shape[1]
    crow = space // CHUNKS
    hrow = crow // 2
    vmem = pl.BlockSpec(memory_space=pltpu.VMEM)
    hbm = pl.BlockSpec(memory_space=pl.ANY)
    dma = pltpu.SemaphoreType.DMA
    hops = depth // 2
    args = (
        slab_rows,
        guess,
        right_side,
        diagonal,
        rates,
        term_source,
        term_target,
        term_left,
        term_right,
        left_factors,
        right_factors,
    )
    out = pl.pallas_call(
        kernel,
        out_shape=pltpu.VMEM((space, space), F32),
        in_specs=[hbm] * len(args),
        out_specs=vmem,
        scratch_shapes=[
            pltpu.VMEM((2, depth, space, space), BF),
            pltpu.VMEM((depth, factors, space, space), BF),
            pltpu.VMEM((terms + 1, space, space), F32),
            pltpu.VMEM((CHUNKS, RING, RING, crow, space), BF),
            pltpu.VMEM((2, CHUNKS, RING, RING, crow, space), BF),
            pltpu.VMEM((CHUNKS, 2, 3, RING, hrow, space), BF),
            pltpu.VMEM((2, CHUNKS, 2, 3, RING, hrow, space), BF),
            pltpu.VMEM((2, CHUNKS, RING - 1, crow, space), BF),
            pltpu.VMEM((CHUNKS, RING - 1, crow, space), BF),
            pltpu.VMEM((CHUNKS, crow, space), F32),
            pltpu.VMEM((factors, space, space), BF),
            pltpu.VMEM((factors, space, space), BF),
            pltpu.VMEM((space, space), F32),
            pltpu.VMEM((space, space), F32),
            pltpu.VMEM((space, space), F32),
            pltpu.VMEM((1, terms), jnp.int32),
            pltpu.VMEM((8, 128), jnp.int32),
            pltpu.SMEM((1,), jnp.int32),
            pltpu.SMEM((1, terms), F32),
            pltpu.SMEM((1, terms), jnp.int32),
            pltpu.SMEM((1, terms), jnp.int32),
            pltpu.SMEM((1, terms), jnp.int32),
            pltpu.SMEM((8, 128), jnp.int32),
            dma((12,)),
            dma((2, CHUNKS, hops, 2)),
            dma((2, CHUNKS, hops, 2)),
            dma((2, CHUNKS, RING)),
            dma((2, CHUNKS, RING)),
            dma((2, CHUNKS, 2, 3)),
            dma((2, CHUNKS, 2, 3)),
            dma((2, CHUNKS, RING - 1)),
            dma((2, CHUNKS, RING - 1)),
        ],
        compiler_params=pltpu.CompilerParams(
            collective_id=0, has_side_effects=True, vmem_limit_bytes=60 * 1024 * 1024
        ),
        cost_estimate=pl.CostEstimate(
            flops=4 * (depth * factors + terms) * space**3,
            bytes_accessed=4 * 1024 * 1024,
            transcendentals=0,
        ),
    )(*args)
    return out.reshape(1, space, space)


def solution(mesh):
    in_specs = (
        P(("row", "col")),
        P(("row", "col"), None, None),
        P(("row", "col"), None, None),
        P(("row", "col"), None, None),
        P("row", "col"),
        P("row", "col"),
        P("row", "col"),
        P("row", "col"),
        P("row", "col"),
        P(),
        P(),
    )
    out_specs = P(("row", "col"), None, None)
    return jax.shard_map(body, mesh=mesh, in_specs=in_specs, out_specs=out_specs, check_vma=False)
```
